512 devices in a mesh: patch: 128 (over z, x_hi, y), head: 4 (over x_lo, core).
Axes of the slice: x: 4 (x_hi: 2, x_lo: 2; x = x_hi * 2 + x_lo), y: 8, z: 8, core: 2. Of those that a mesh axis runs over, the one named last changes fastest.
Arguments:
- queries: bfloat16 [32768, 3072], P(('patch', 'head')), may hold values from -16 to 16
- keys: bfloat16 [32768, 3072], P(('patch', 'head')), may hold values from -5 to 5
- values: bfloat16 [32768, 3072], P(('patch', 'head')), may hold values from -6 to 6
Outputs:
- attended: bfloat16 [32768, 3072], P(('patch', 'head'))
The draws below stay inside these ranges and needn't reach their ends.
All inputs are finite; a program needn't handle non-finite values.
Results may differ from the reference program's by a relative error of at most 0.0085.
Values may be sent and summed in bfloat16 or wider, within the bound.
A program may use at most 128 MiB of HBM per device.

```python
import math
import jax
import jax.numpy as jnp
from jax import lax

H = 24
HD = 128
D = 3072
POOL = 16
TOKENS = 32768
KEYS = 2048


def draw_queries(key, part):
    key = jax.random.fold_in(key, 3)
    result = 4.0 * jax.random.truncated_normal(key, -4.0, 4.0, (TOKENS, D), jnp.float32)
    return result.astype(jnp.bfloat16)


def draw_keys(key, part):
    key = jax.random.fold_in(key, 7)
    result = jax.random.truncated_normal(key, -5.0, 5.0, (TOKENS, D), jnp.float32)
    return result.astype(jnp.bfloat16)


def shard_levels(rng, dims, shards, smallest, largest):
    def one(position, blocks):
        heights = jax.random.uniform(jax.random.fold_in(jax.random.fold_in(rng, 6), position), (blocks,), jnp.float32, smallest / len(shards), largest / len(shards))
        return jnp.repeat(jnp.exp(heights), dims[position] // blocks).reshape((-1,) + (1,) * (len(dims) - position - 1))

    factor_of = one(*shards[0])
    for cut in shards[1:]:
        factor_of = factor_of * one(*cut)
    return factor_of


def noise(stream_key, shape, width, bound, cuts=(), dtype=jnp.bfloat16):
    level = shard_levels(stream_key, shape, cuts, -0.22, 0.18) if cuts else 1.0
    entries = jax.random.normal(stream_key, shape, jnp.float32) * width * level
    return jnp.minimum(jnp.maximum(entries, -bound), bound).astype(dtype)


def setup_inputs(seed: int = 0) -> dict:
    streams_of = jax.random.split(jax.random.key(seed), 4)
    return {
        "queries": draw_queries(jax.random.fold_in(streams_of[3], 71), 0),
        "keys": draw_keys(jax.random.fold_in(streams_of[3], 71), 0),
        "values": noise(streams_of[2], (TOKENS, D), 1.0, 6.0, ((0, 512),)),
    }


def pool_tokens(array):
    grouped = array.reshape(array.shape[0] // POOL, POOL, array.shape[1]).astype(jnp.float32)
    return lax.optimization_barrier(jnp.mean(grouped, axis=1)).astype(jnp.bfloat16)

def reference(queries, keys, values):
    pooled_keys = pool_tokens(keys)
    pooled_values = pool_tokens(values)
    block_rows = math.gcd(TOKENS, 4096)
    score_scale = HD ** (-0.5)
    head_queries = queries.reshape(TOKENS // block_rows, block_rows, H, HD).transpose(2, 0, 1, 3)
    head_keys = pooled_keys.reshape(KEYS, H, HD).transpose(1, 0, 2)
    head_values = pooled_values.reshape(KEYS, H, HD).transpose(1, 0, 2)

    def one_head(operands):
        query_blocks, key_rows, value_rows = operands

        def one_block(query_rows):
            scores = jnp.dot(query_rows, key_rows.T, preferred_element_type=jnp.float32) * score_scale
            peak = lax.optimization_barrier(jnp.max(scores, axis=1, keepdims=True))
            exponent = jnp.exp(scores - peak)
            totals = lax.optimization_barrier(jnp.sum(exponent, axis=1, keepdims=True))
            weights = exponent.astype(jnp.bfloat16)
            mixed = jnp.dot(weights, value_rows, preferred_element_type=jnp.float32) / totals
            power = lax.optimization_barrier(jnp.mean(mixed * mixed, axis=1, keepdims=True))
            return (mixed / jnp.sqrt(power + 1e-06)).astype(jnp.bfloat16)
        return lax.map(one_block, query_blocks)
    outputs = lax.map(one_head, (head_queries, head_keys, head_values))
    return outputs.transpose(1, 2, 0, 3).reshape(TOKENS, H * HD)
```

```python
import functools

import jax
import jax.numpy as jnp
from jax import lax
from jax.experimental import pallas as pl
from jax.experimental.pallas import tpu as pltpu
from jax.sharding import PartitionSpec as P

HD = 128
POOL = 16
EPS = 1e-6
X, Y, Z, C = 4, 8, 8, 2
MESH = pl.DeviceIdType.MESH
ORDER = (4, 3, 5, 2, 6, 1, 7, 0)
SLOT = {dz: slot for slot, dz in enumerate(ORDER)}


def ring_steps(n):
    full = [(s, t) for s in range(n // 2 - 1) for t in range(2)]
    return full + [(n // 2 - 1, 0)]


def kernel(
    q_hbm, k_hbm, v_hbm, o_hbm,
    kv_in, send_kv, recv_kv, buf1, buf2, qbuf, obuf,
    local_sem, zk_s, zk_r, zq_s, zq_r,
    x1_s, x1_r, yr_s, yr_r, yl_s, yl_r, c1_s, c1_r,
    y2_s, y2_r, xr_s, xr_r, xl_s, xl_r, c2_s, c2_r,
    o_s, o_r,
):
    tokens, width = q_hbm.shape
    cols = width // Z
    heads = cols // HD
    groups = tokens // POOL
    xh = X // 2
    patch, head = lax.axis_index("patch"), lax.axis_index("head")
    y = lax.rem(patch, Y)
    x_hi = lax.rem(lax.div(patch, Y), xh)
    z = lax.div(patch, Y * xh)
    x = x_hi * 2 + lax.div(head, C)
    c = lax.rem(head, C)

    def at(xx, yy, zz, cc):
        return ((zz * xh + lax.div(xx, 2)) * Y + yy, lax.rem(xx, 2) * C + cc)

    def plus(a, d, n):
        return lax.rem(a + d + n, n)

    def z_at(dz):
        return at(x, y, plus(z, dz, Z), c)

    def x_at(dx):
        return at(plus(x, dx, X), y, z, c)

    def y_at(dy):
        return at(x, plus(y, dy, Y), z, c)

    sibling = at(x, y, z, C - 1 - c)

    def remote(src, dst, send, recv, device):
        return pltpu.make_async_remote_copy(
            src_ref=src, dst_ref=dst, send_sem=send, recv_sem=recv,
            device_id=device, device_id_type=MESH,
        )

    barrier = pltpu.get_barrier_semaphore()
    peers = [z_at(d) for d in range(1, Z)] + [x_at(d) for d in range(1, X)]
    peers += [y_at(d) for d in range(1, Y)] + ([sibling] if C > 1 else [])
    for peer in peers:
        pl.semaphore_signal(barrier, inc=1, device_id=peer, device_id_type=MESH)

    load_k = pltpu.make_async_copy(k_hbm, kv_in.at[pl.ds(0, tokens)], local_sem.at[0])
    load_v = pltpu.make_async_copy(v_hbm, kv_in.at[pl.ds(tokens, tokens)], local_sem.at[1])
    own_q = pltpu.make_async_copy(
        q_hbm.at[:, pl.ds(pl.multiple_of(z * cols, HD), cols)], qbuf.at[SLOT[0]], local_sem.at[2]
    )
    load_k.start()
    load_v.start()
    own_q.start()

    row = lax.broadcasted_iota(jnp.int32, (2 * groups, 2 * tokens), 0)
    col = lax.broadcasted_iota(jnp.int32, (2 * groups, 2 * tokens), 1)
    mean = jnp.where(lax.div(col, POOL) == row, 1.0 / POOL, 0.0).astype(jnp.bfloat16)
    load_k.wait()
    load_v.wait()
    pooled = jnp.dot(mean, kv_in[...], preferred_element_type=jnp.float32)
    pad = jnp.zeros((32 - heads * 2 * groups, HD), jnp.float32)
    for zz in range(Z):
        pieces = [pooled[:, (zz * heads + j) * HD : (zz * heads + j + 1) * HD] for j in range(heads)]
        send_kv[zz] = jnp.concatenate(pieces + [pad], axis=0).astype(jnp.bfloat16)
    recv_kv[z] = send_kv[z]

    pl.semaphore_wait(barrier, len(peers))

    waits = []
    kv_copies, q_copies = [], []
    for dz in ORDER[:-1]:
        copy = remote(
            send_kv.at[plus(z, dz, Z)], recv_kv.at[z], zk_s.at[dz - 1], zk_r.at[dz - 1], z_at(dz)
        )
        copy.start()
        waits.append(copy.wait_send)
    for dz in ORDER[:-1]:
        columns = pl.ds(pl.multiple_of(plus(z, dz, Z) * cols, HD), cols)
        copy = remote(
            q_hbm.at[:, columns], qbuf.at[SLOT[dz]], zq_s.at[dz - 1], zq_r.at[dz - 1], z_at(dz)
        )
        copy.start()
        waits.append(copy.wait_send)
        q_copies.append(copy)
    for dz in ORDER[:-1]:
        remote(
            send_kv.at[0], recv_kv.at[plus(z, -dz, Z)], zk_s.at[dz - 1], zk_r.at[dz - 1], z_at(dz)
        ).wait_recv()

    rows = 2 * heads * Z * groups
    row = lax.broadcasted_iota(jnp.int32, (rows, Z * 32), 0)
    col = lax.broadcasted_iota(jnp.int32, (rows, Z * 32), 1)
    which, place = lax.div(row, Z * groups), lax.rem(row, Z * groups)
    wanted = (
        lax.div(place, groups) * 32
        + lax.rem(which, heads) * (2 * groups)
        + lax.div(which, heads) * groups
        + lax.rem(place, groups)
    )
    pick = jnp.where(col == wanted, 1.0, 0.0).astype(jnp.bfloat16)
    block = jnp.dot(pick, recv_kv[...].reshape(Z * 32, HD), preferred_element_type=jnp.float32)
    block = block.astype(jnp.bfloat16).reshape(2 * heads, 2, 16, HD)
    buf1[y, c, x] = block[:, 0]
    buf2[x, c, y] = block[:, 1]

    for dx in range(1, X):
        ref = buf1.at[y, c, x]
        copy = remote(ref, ref, x1_s.at[dx - 1], x1_r.at[dx - 1], x_at(dx))
        copy.start()
        waits.append(copy.wait_send)
    for dy in (4, 3, 5, 2, 6, 1, 7) if Y == 8 else range(1, Y):
        ref = buf2.at[x, c, y]
        copy = remote(ref, ref, y2_s.at[dy - 1], y2_r.at[dy - 1], y_at(dy))
        copy.start()
        waits.append(copy.wait_send)

    half1, half2 = X // 2, Y // 2

    def piece1(i, t, core):
        return buf1.at[plus(y, i, Y), core, pl.ds(t * half1, half1)]

    def piece2(i, t, core):
        return buf2.at[plus(x, i, X), core, pl.ds(t * half2, half2)]

    def ring(n, piece, where, sr, rr, sl, rl, cs, cr):
        right = ring_steps(n)
        arrivals = []

        def share(i, t, number):
            if C > 1:
                copy = remote(piece(i, t, c), piece(i, t, c), cs.at[number], cr.at[number], sibling)
                copy.start()
                waits.append(copy.wait_send)
                other = remote(
                    piece(i, t, 1 - c), piece(i, t, 1 - c), cs.at[number], cr.at[number], sibling
                )
                arrivals.append(other.wait_recv)

        def send(step, t, way):
            i = -step * way
            ref = piece(i, t, c)
            s, r = (sr, rr) if way == 1 else (sl, rl)
            copy = remote(ref, ref, s.at[2 * step + (t if way == 1 else 1 - t)],
                          r.at[2 * step + (t if way == 1 else 1 - t)], where(way))
            copy.start()
            waits.append(copy.wait_send)

        def begin():
            for k in range(2):
                for way in (1, -1):
                    t = k if way == 1 else 1 - k
                    if (0, k) in right:
                        send(0, t, way)
            for t in range(2):
                share(0, t, t)

        def step(number):
            s, k = right[number]
            for way in (1, -1):
                t = k if way == 1 else 1 - k
                i = -(s + 1) * way
                ref = piece(i, t, c)
                ss, rr_ = (sr, rr) if way == 1 else (sl, rl)
                remote(ref, ref, ss.at[2 * s + k], rr_.at[2 * s + k], where(way)).wait_recv()
                if (s + 1, k) in right:
                    send(s + 1, t, way)
                share(i, t, 2 + 2 * number + (0 if way == 1 else 1))

        return begin, [functools.partial(step, number) for number in range(len(right))], arrivals

    begin1, steps1, arrivals1 = ring(Y, piece1, y_at, yr_s, yr_r, yl_s, yl_r, c1_s, c1_r)
    begin2, steps2, arrivals2 = ring(X, piece2, x_at, xr_s, xr_r, xl_s, xl_r, c2_s, c2_r)

    for dx in range(1, X):
        ref = buf1.at[y, c, plus(x, -dx, X)]
        remote(ref, ref, x1_s.at[dx - 1], x1_r.at[dx - 1], x_at(dx)).wait_recv()
    begin1()
    for dy in range(1, Y):
        ref = buf2.at[x, c, plus(y, -dy, Y)]
        remote(ref, ref, y2_s.at[dy - 1], y2_r.at[dy - 1], y_at(dy)).wait_recv()
    begin2()
    todo1, todo2 = list(steps1), list(steps2)
    while todo1 or todo2:
        for _ in range(2):
            if todo1:
                todo1.pop(0)()
        if todo2:
            todo2.pop(0)()

    own_q.wait()
    for copy in q_copies:
        copy.wait_recv()
    for wait in arrivals1 + arrivals2:
        wait()

    scale = HD ** (-0.5)
    part = Z // 2
    rows1, rows2 = Y * C * X * 16, X * C * Y * 16

    def output(slot, j):
        dz = ORDER[slot]
        column = pl.ds(pl.multiple_of(j * HD, HD), HD)
        away = pl.ds(pl.multiple_of(z * cols + j * HD, HD), HD)
        src, dst = obuf.at[slot, :, column], o_hbm.at[:, away]
        number = slot * heads + j
        if dz == 0:
            return pltpu.make_async_copy(src, dst, o_s.at[number])
        return remote(src, dst, o_s.at[number], o_r.at[number], z_at(-dz))

    for half in range(2):
        slots = range(half * part, (half + 1) * part)

        def one_head(j, carry):
            column = pl.ds(pl.multiple_of(j * HD, HD), HD)
            query = qbuf[half * part : (half + 1) * part, :, column].reshape(part * tokens, HD)
            across = (((1,), (1,)), ((), ()))
            key1 = buf1[:, :, :, j].reshape(rows1, HD)
            key2 = buf2[:, :, :, j].reshape(rows2, HD)
            scores1 = lax.dot_general(query, key1, across, preferred_element_type=jnp.float32)
            scores2 = lax.dot_general(query, key2, across, preferred_element_type=jnp.float32)
            peak = jnp.maximum(
                jnp.max(scores1, axis=1, keepdims=True), jnp.max(scores2, axis=1, keepdims=True)
            )
            weights1 = jnp.exp((scores1 - peak) * scale).astype(jnp.bfloat16)
            weights2 = jnp.exp((scores2 - peak) * scale).astype(jnp.bfloat16)
            value1 = buf1[:, :, :, heads + j].reshape(rows1, HD)
            value2 = buf2[:, :, :, heads + j].reshape(rows2, HD)
            value1 = jnp.concatenate([value1, jnp.ones_like(value1)], axis=1)
            value2 = jnp.concatenate([value2, jnp.ones_like(value2)], axis=1)
            both = jnp.dot(weights1, value1, preferred_element_type=jnp.float32)
            both += jnp.dot(weights2, value2, preferred_element_type=jnp.float32)
            mixed = both[:, :HD] / both[:, HD:]
            power = jnp.mean(mixed * mixed, axis=1, keepdims=True)
            normed = (mixed * lax.rsqrt(power + EPS)).astype(jnp.bfloat16)
            obuf[half * part : (half + 1) * part, :, column] = normed.reshape(part, tokens, HD)
            for slot in slots:
                output(slot, j).start()
            return carry

        lax.fori_loop(0, heads, one_head, 0)

    for slot in range(Z):
        for j in range(heads):
            copy = output(slot, j)
            if ORDER[slot] == 0:
                copy.wait()
            else:
                copy.wait_send()
    for slot in range(Z):
        dz = ORDER[slot]
        if dz:
            for j in range(heads):
                away = pl.ds(pl.multiple_of(plus(z, dz, Z) * cols + j * HD, HD), HD)
                number = slot * heads + j
                remote(
                    obuf.at[slot, :, pl.ds(j * HD, HD)], o_hbm.at[:, away],
                    o_s.at[number], o_r.at[number], z_at(-dz),
                ).wait_recv()
    for wait in waits:
        wait()


def shards(queries, keys, values):
    tokens, width = queries.shape
    cols = width // Z
    heads = cols // HD
    dma = pltpu.SemaphoreType.DMA
    bf16 = jnp.bfloat16
    n1, n2 = 2 * Y, 2 * X
    sems = [3, Z - 1, Z - 1, Z - 1, Z - 1]
    sems += [X - 1, X - 1] + [Y] * 4 + [n1, n1]
    sems += [Y - 1, Y - 1] + [X] * 4 + [n2, n2]
    sems += [Z * heads, Z * heads]
    return pl.pallas_call(
        kernel,
        out_shape=jax.ShapeDtypeStruct(queries.shape, bf16),
        in_specs=[pl.BlockSpec(memory_space=pl.ANY)] * 3,
        out_specs=pl.BlockSpec(memory_space=pl.ANY),
        scratch_shapes=[
            pltpu.VMEM((2 * tokens, width), bf16),
            pltpu.VMEM((Z, 32, HD), bf16),
            pltpu.VMEM((Z, 32, HD), bf16),
            pltpu.VMEM((Y, C, X, 2 * heads, 16, HD), bf16),
            pltpu.VMEM((X, C, Y, 2 * heads, 16, HD), bf16),
            pltpu.VMEM((Z, tokens, cols), bf16),
            pltpu.VMEM((Z, tokens, cols), bf16),
        ]
        + [dma((max(n, 1),)) for n in sems],
        compiler_params=pltpu.CompilerParams(
            collective_id=0, has_side_effects=True, vmem_limit_bytes=48 * 2**20
        ),
    )(queries, keys, values)


def solution(mesh):
    spec = P(("patch", "head"), None)
    return jax.shard_map(
        shards, mesh=mesh, in_specs=(spec, spec, spec), out_specs=spec, check_vma=False
    )
```

```python
import functools

import jax
import jax.numpy as jnp
from jax import lax
from jax.experimental import pallas as pl
from jax.experimental.pallas import tpu as pltpu
from jax.sharding import PartitionSpec as P

HD = 128
POOL = 16
EPS = 1e-6
VMEM_BYTES = (64 * 1024 - 10880) * 2**10
X, Y, Z, C = 4, 8, 8, 2
MESH = pl.DeviceIdType.MESH
ORDER = (4, 3, 5, 2, 6, 1, 7, 0)
SLOT = {dz: slot for slot, dz in enumerate(ORDER)}


FIRST = 5
GROUPS = (4, 3)
THROTTLE1 = True
PLAN = ("b", "s", "t0", "n", "t1", "f", "g0", "e", "g1", "c")
HEADS_FIRST = True
CHUNK = 512


def kernel(
    q_hbm, k_hbm, v_hbm, o_hbm,
    kv_in, send_kv, recv_kv, kv_buf, qbuf, obuf,
    local_sem, zk_s, zk_r, zq_s, zq_r, y2_s, y2_r, x2_s, x2_r, c2_s, c2_r,
    x1_s, x1_r, y1_s, y1_r, c1_s, c1_r, o_s, o_r,
):
    tokens, width = q_hbm.shape
    cols = width // Z
    heads = cols // HD
    groups = tokens // POOL
    xh = X // 2
    patch, head = lax.axis_index("patch"), lax.axis_index("head")
    y = lax.rem(patch, Y)
    x_hi = lax.rem(lax.div(patch, Y), xh)
    z = lax.div(patch, Y * xh)
    x = x_hi * 2 + lax.div(head, C)
    c = lax.rem(head, C)

    def at(xx, yy, zz, cc):
        return ((zz * xh + lax.div(xx, 2)) * Y + yy, lax.rem(xx, 2) * C + cc)

    def plus(a, d, n):
        return lax.rem(a + d + n, n)

    def z_at(dz):
        return at(x, y, plus(z, dz, Z), c)

    def x_at(dx):
        return at(plus(x, dx, X), y, z, c)

    def y_at(dy):
        return at(x, plus(y, dy, Y), z, c)

    sibling = at(x, y, z, C - 1 - c)

    def remote(src, dst, send, recv, device):
        return pltpu.make_async_remote_copy(
            src_ref=src, dst_ref=dst, send_sem=send, recv_sem=recv,
            device_id=device, device_id_type=MESH,
        )

    barrier = pltpu.get_barrier_semaphore()
    peers = [z_at(d) for d in range(1, Z)] + [x_at(d) for d in range(1, X)]
    peers += [y_at(d) for d in range(1, Y)] + ([sibling] if C > 1 else [])
    load_k = pltpu.make_async_copy(k_hbm, kv_in.at[pl.ds(0, tokens)], local_sem.at[0])
    load_v = pltpu.make_async_copy(v_hbm, kv_in.at[pl.ds(tokens, tokens)], local_sem.at[1])
    own_q = pltpu.make_async_copy(
        q_hbm.at[:, pl.ds(pl.multiple_of(z * cols, HD), cols)], qbuf.at[SLOT[0]], local_sem.at[2]
    )
    load_k.start()
    load_v.start()

    for peer in peers:
        pl.semaphore_signal(barrier, inc=1, device_id=peer, device_id_type=MESH)

    own_q.start()

    row = lax.broadcasted_iota(jnp.int32, (2 * groups, 2 * tokens), 0)
    col = lax.broadcasted_iota(jnp.int32, (2 * groups, 2 * tokens), 1)
    mean = jnp.where(lax.div(col, POOL) == row, 1.0 / POOL, 0.0).astype(jnp.bfloat16)
    load_k.wait()
    load_v.wait()
    pooled = jnp.dot(mean, kv_in[...], preferred_element_type=jnp.float32)
    pad = jnp.zeros((32 - heads * 2 * groups, HD), jnp.float32)
    for zz in range(Z):
        pieces = [pooled[:, (zz * heads + j) * HD : (zz * heads + j + 1) * HD] for j in range(heads)]
        send_kv[zz] = jnp.concatenate(pieces + [pad], axis=0).astype(jnp.bfloat16)
    recv_kv[z] = send_kv[z]

    pl.semaphore_wait(barrier, len(peers))

    def wait(ref, sem):
        pltpu.make_async_copy(ref, ref, sem).wait()

    for dz in ORDER[:-1]:
        remote(send_kv.at[plus(z, dz, Z)], recv_kv.at[z], zk_s, zk_r, z_at(dz)).start()
    for dz in ORDER[:-1]:
        columns = pl.ds(pl.multiple_of(plus(z, dz, Z) * cols, HD), cols)
        remote(q_hbm.at[:, columns], qbuf.at[SLOT[dz]], zq_s, zq_r, z_at(dz)).start()
    wait(recv_kv.at[pl.ds(0, Z - 1)], zk_r)

    pieces = 4 * heads
    row = lax.broadcasted_iota(jnp.int32, (pieces * 16, Z * 32), 0)
    col = lax.broadcasted_iota(jnp.int32, (pieces * 16, Z * 32), 1)
    piece = lax.div(row, 16)
    place = lax.rem(lax.div(piece, heads), 2) * 16 + lax.rem(row, 16)
    wanted = (
        lax.div(place, groups) * 32
        + lax.rem(piece, heads) * (2 * groups)
        + lax.div(piece, 2 * heads) * groups
        + lax.rem(place, groups)
    )
    pick = jnp.where(col == wanted, 1.0, 0.0).astype(jnp.bfloat16)
    block = jnp.dot(pick, recv_kv[...].reshape(Z * 32, HD), preferred_element_type=jnp.float32)
    kv_buf[:, x, c, y] = block.astype(jnp.bfloat16).reshape(pieces, 16, HD)

    def go(ref, send, recv, device):
        remote(ref, ref, send, recv, device).start()

    first = pl.ds(0, FIRST)
    second = [pl.ds(FIRST + sum(GROUPS[:k]), GROUPS[k]) for k in range(len(GROUPS))]
    far_y = (4, 3, 5, 2, 6, 1, 7) if Y == 8 else tuple(range(1, Y))
    far_x = (2, 1, 3) if X == 4 else tuple(range(1, X))
    low, high = pl.ds(0, X // 2), pl.ds(X // 2, X // 2)

    def column(dy, some=slice(None)):
        return kv_buf.at[first, some, c, plus(y, dy, Y)]

    def line(k, dx):
        return kv_buf.at[second[k], plus(x, dx, X), c]

    def columns1(n):
        return kv_buf.at[first, :, 0, pl.ds(0, n)]

    def lines2(k, n):
        return kv_buf.at[second[k], pl.ds(0, n), 0]

    def share(ref, send, recv):
        if C > 1:
            go(ref, send, recv, sibling)

    def pushes2(k):
        return kv_buf.at[second[k], 0, 0, pl.ds(0, Y - 1)]

    def begin():
        for dx in far_x:
            go(kv_buf.at[first, x, c, y], x1_s, x1_r, x_at(dx))
        for k in range(len(GROUPS)):
            if k:
                wait(pushes2(k - 1), y2_s.at[k - 1])
            for dy in far_y:
                go(kv_buf.at[second[k], x, c, y], y2_s.at[k], y2_r.at[k], y_at(dy))

    def spread1():
        wait(kv_buf.at[first, pl.ds(0, X - 1), 0, 0], x1_r)
        for dy in (2, -2):
            go(column(0), y1_s.at[0], y1_r.at[0], y_at(dy))
        if not THROTTLE1:
            near1()
        share(column(0), c1_s, c1_r)

    def near1():
        if THROTTLE1:
            wait(columns1(2), y1_s.at[0])
        for dy in (1, -1):
            go(column(0), y1_s.at[1], y1_r.at[1], y_at(dy))

    def spread2(k):
        wait(pushes2(k), y2_r.at[k])
        for dx in far_x:
            go(line(k, 0), x2_s.at[k], x2_r.at[k, 1 if 2 * dx == X else 0], x_at(dx))
        share(line(k, 0), c2_s.at[k], c2_r.at[k])

    def forward1():
        wait(columns1(2), y1_r.at[0])
        for way, some in ((1, low), (-1, high)):
            go(column(-2 * way), y1_s.at[1], y1_r.at[2], y_at(way))
            go(column(-2 * way, some), y1_s.at[1], y1_r.at[3], y_at(2 * way))
        for dy in (2, -2):
            share(column(dy), c1_s, c1_r)
        wait(columns1(2), y1_r.at[1])
        for dy in (1, -1):
            share(column(dy), c1_s, c1_r)

    def finish1():
        wait(columns1(2), y1_r.at[2])
        for dy in (3, -3):
            share(column(dy), c1_s, c1_r)
        wait(columns1(1), y1_r.at[3])
        share(column(4), c1_s, c1_r)

    def finish2(k):
        near = [dx for dx in far_x if 2 * dx != X]
        if near:
            wait(lines2(k, len(near)), x2_r.at[k, 0])
        for dx in near:
            share(line(k, -dx), c2_s.at[k], c2_r.at[k])
        wait(lines2(k, 1), x2_r.at[k, 1])
        share(line(k, -X // 2), c2_s.at[k], c2_r.at[k])

    def complete():
        if C > 1:
            for k in range(len(GROUPS)):
                wait(lines2(k, X), c2_r.at[k])
            wait(columns1(Y), c1_r)

    scale = HD ** (-0.5)
    part = Z // 2
    keys_all = 2 * X * C * Y * 16

    def output(slot, j):
        dz = ORDER[slot]
        column = pl.ds(pl.multiple_of(j * HD, HD), HD)
        away = pl.ds(pl.multiple_of(z * cols + j * HD, HD), HD)
        src, dst = obuf.at[slot, :, column], o_hbm.at[:, away]
        if dz == 0:
            return pltpu.make_async_copy(src, dst, local_sem.at[3])
        return remote(src, dst, o_s, o_r, z_at(-dz))

    def attend(j, half):
        here = slice(half * part, (half + 1) * part)
        column = slice(j * HD, (j + 1) * HD)
        query = qbuf[here, :, column].reshape(part * tokens, HD)
        keys = [kv_buf[k * heads + j].reshape(keys_all // 2, HD) for k in (0, 1)]
        values = [kv_buf[k * heads + j].reshape(keys_all // 2, HD) for k in (2, 3)]
        values = [jnp.concatenate([v, jnp.ones_like(v)], axis=1) for v in values]
        across = (((1,), (1,)), ((), ()))
        peak, both = None, None
        for k in range(0, keys_all, CHUNK):
            part_of, at_row = divmod(k, keys_all // 2)
            rows = slice(at_row, at_row + CHUNK)
            scores = lax.dot_general(
                query, keys[part_of][rows], across, preferred_element_type=jnp.float32
            )
            new = jnp.max(scores, axis=1, keepdims=True)
            if k:
                new = jnp.maximum(peak, new)
            weights = jnp.exp((scores - new) * scale).astype(jnp.bfloat16)
            term = jnp.dot(weights, values[part_of][rows], preferred_element_type=jnp.float32)
            both = both * jnp.exp((peak - new) * scale) + term if k else term
            peak = new
        mixed = both[:, :HD] / both[:, HD:]
        power = jnp.mean(mixed * mixed, axis=1, keepdims=True)
        normed = (mixed * lax.rsqrt(power + EPS)).astype(jnp.bfloat16)
        obuf[here, :, column] = normed.reshape(part, tokens, HD)
        for slot in range(Z)[here]:
            output(slot, j).start()

    def queries_here():
        own_q.wait()
        wait(qbuf.at[pl.ds(0, Z - 1)], zq_r)

    steps = {
        "b": begin, "s": spread1, "t": spread2, "f": forward1, "e": finish1, "g": finish2, "n": near1,
        "c": complete,
    }
    for word in PLAN:
        if word != "n" or THROTTLE1:
            steps[word[0]](*(int(digit) for digit in word[1:]))
    queries_here()
    units = [(j, half) for j in range(heads) for half in range(2)]
    for j, half in units if HEADS_FIRST else sorted(units, key=lambda unit: unit[1]):
        attend(j, half)

    mine = obuf.at[SLOT[0]]
    wait(mine, local_sem.at[3])
    wait(obuf.at[pl.ds(0, Z - 1)], o_s)
    wait(obuf.at[pl.ds(0, Z - 1)], o_r)
    wait(send_kv.at[pl.ds(0, Z - 1)], zk_s)
    wait(qbuf.at[pl.ds(0, Z - 1)], zq_s)
    wait(kv_buf.at[first, pl.ds(0, X - 1), 0, 0], x1_s)
    if THROTTLE1:
        wait(columns1(5), y1_s.at[1])
    else:
        wait(columns1(2), y1_s.at[0])
        wait(columns1(5), y1_s.at[1])
    wait(pushes2(len(GROUPS) - 1), y2_s.at[len(GROUPS) - 1])
    for k in range(len(GROUPS)):
        wait(lines2(k, X - 1), x2_s.at[k])
        if C > 1:
            wait(lines2(k, X), c2_s.at[k])
    if C > 1:
        wait(columns1(Y), c1_s)


def shards(queries, keys, values):
    tokens, width = queries.shape
    cols = width // Z
    heads = cols // HD
    dma = pltpu.SemaphoreType.DMA
    bf16 = jnp.bfloat16
    return pl.pallas_call(
        kernel,
        out_shape=jax.ShapeDtypeStruct(queries.shape, bf16),
        in_specs=[pl.BlockSpec(memory_space=pltpu.HBM)] * 3,
        out_specs=pl.BlockSpec(memory_space=pl.ANY),
        scratch_shapes=[
            pltpu.VMEM((2 * tokens, width), bf16),
            pltpu.VMEM((Z, 32, HD), bf16),
            pltpu.VMEM((Z, 32, HD), bf16),
            pltpu.VMEM((4 * heads, X, C, Y, 16, HD), bf16),
            pltpu.VMEM((Z, tokens, cols), bf16),
            pltpu.VMEM((Z, tokens, cols), bf16),
        ]
        + [dma((4,))]
        + [dma] * 4
        + [dma((len(GROUPS),))] * 3
        + [dma((len(GROUPS), 2))]
        + [dma((len(GROUPS),))] * 2
        + [dma] * 2
        + [dma((2,)), dma((4,))]
        + [dma] * 4,
        compiler_params=pltpu.CompilerParams(
            collective_id=0, has_side_effects=True, vmem_limit_bytes=VMEM_BYTES
        ),
    )(queries, keys, values)


def solution(mesh):
    spec = P(("patch", "head"), None)
    return jax.shard_map(
        shards, mesh=mesh, in_specs=(spec, spec, spec), out_specs=spec, check_vma=False
    )
```

```python
import functools

import jax
import jax.numpy as jnp
from jax import lax
from jax.experimental import pallas as pl
from jax.experimental.pallas import tpu as pltpu
from jax.sharding import PartitionSpec as P

HD = 128
POOL = 16
EPS = 1e-6
VMEM_BYTES = (64 * 1024 - 10880) * 2**10
X, Y, Z, C = 4, 8, 8, 2
MESH = pl.DeviceIdType.MESH
ORDER = (4, 3, 5, 2, 6, 1, 7, 0)
SLOT = {dz: slot for slot, dz in enumerate(ORDER)}


FIRST = 5
GROUPS = (4, 3)
THROTTLE1 = True
PLAN = ("b", "s", "t0", "n", "t1", "f", "g0", "e", "g1", "c")
HEADS_FIRST = True
CHUNK = 512


def kernel(
    q_hbm, k_hbm, v_hbm, o_hbm,
    kv_in, send_kv, recv_kv, kv_buf, qbuf, obuf,
    local_sem, zk_s, zk_r, zq_s, zq_r, y2_s, y2_r, x2_s, x2_r, c2_s, c2_r,
    x1_s, x1_r, y1_s, y1_r, c1_s, c1_r, o_s, o_r,
):
    tokens, width = q_hbm.shape
    cols = width // Z
    heads = cols // HD
    groups = tokens // POOL
    xh = X // 2
    patch, head = lax.axis_index("patch"), lax.axis_index("head")
    y = lax.rem(patch, Y)
    x_hi = lax.rem(lax.div(patch, Y), xh)
    z = lax.div(patch, Y * xh)
    x = x_hi * 2 + lax.div(head, C)
    c = lax.rem(head, C)

    def at(xx, yy, zz, cc):
        return ((zz * xh + lax.div(xx, 2)) * Y + yy, lax.rem(xx, 2) * C + cc)

    def plus(a, d, n):
        return lax.rem(a + d + n, n)

    def z_at(dz):
        return at(x, y, plus(z, dz, Z), c)

    def x_at(dx):
        return at(plus(x, dx, X), y, z, c)

    def y_at(dy):
        return at(x, plus(y, dy, Y), z, c)

    sibling = at(x, y, z, C - 1 - c)

    def remote(src, dst, send, recv, device):
        return pltpu.make_async_remote_copy(
            src_ref=src, dst_ref=dst, send_sem=send, recv_sem=recv,
            device_id=device, device_id_type=MESH,
        )

    barrier = pltpu.get_barrier_semaphore()
    peers = [z_at(d) for d in range(1, Z)] + [x_at(d) for d in range(1, X)]
    peers += [y_at(d) for d in range(1, Y)] + ([sibling] if C > 1 else [])
    load_k = pltpu.make_async_copy(k_hbm, kv_in.at[pl.ds(0, tokens)], local_sem.at[0])
    load_v = pltpu.make_async_copy(v_hbm, kv_in.at[pl.ds(tokens, tokens)], local_sem.at[1])
    own_q = pltpu.make_async_copy(
        q_hbm.at[:, pl.ds(pl.multiple_of(z * cols, HD), cols)], qbuf.at[SLOT[0]], local_sem.at[2]
    )
    load_k.start()
    load_v.start()

    for peer in peers:
        pl.semaphore_signal(barrier, inc=1, device_id=peer, device_id_type=MESH)

    own_q.start()

    row = lax.broadcasted_iota(jnp.int32, (2 * groups, 2 * tokens), 0)
    col = lax.broadcasted_iota(jnp.int32, (2 * groups, 2 * tokens), 1)
    mean = jnp.where(lax.div(col, POOL) == row, 1.0 / POOL, 0.0).astype(jnp.bfloat16)
    load_k.wait()
    load_v.wait()
    pooled = jnp.dot(mean, kv_in[...], preferred_element_type=jnp.float32)
    pad = jnp.zeros((32 - heads * 2 * groups, HD), jnp.float32)
    for zz in range(Z):
        pieces = [pooled[:, (zz * heads + j) * HD : (zz * heads + j + 1) * HD] for j in range(heads)]
        send_kv[zz] = jnp.concatenate(pieces + [pad], axis=0).astype(jnp.bfloat16)
    recv_kv[z] = send_kv[z]

    pl.semaphore_wait(barrier, len(peers))

    def wait(ref, sem):
        pltpu.make_async_copy(ref, ref, sem).wait()

    for dz in ORDER[:-1]:
        remote(send_kv.at[plus(z, dz, Z)], recv_kv.at[z], zk_s, zk_r, z_at(dz)).start()
    for dz in ORDER[:-1]:
        columns = pl.ds(pl.multiple_of(plus(z, dz, Z) * cols, HD), cols)
        remote(q_hbm.at[:, columns], qbuf.at[SLOT[dz]], zq_s, zq_r, z_at(dz)).start()
    wait(recv_kv.at[pl.ds(0, Z - 1)], zk_r)

    pieces = 4 * heads
    row = lax.broadcasted_iota(jnp.int32, (pieces * 16, Z * 32), 0)
    col = lax.broadcasted_iota(jnp.int32, (pieces * 16, Z * 32), 1)
    piece = lax.div(row, 16)
    place = lax.rem(lax.div(piece, heads), 2) * 16 + lax.rem(row, 16)
    wanted = (
        lax.div(place, groups) * 32
        + lax.rem(piece, heads) * (2 * groups)
        + lax.div(piece, 2 * heads) * groups
        + lax.rem(place, groups)
    )
    pick = jnp.where(col == wanted, 1.0, 0.0).astype(jnp.bfloat16)
    block = jnp.dot(pick, recv_kv[...].reshape(Z * 32, HD), preferred_element_type=jnp.float32)
    kv_buf[:, x, c, y] = block.astype(jnp.bfloat16).reshape(pieces, 16, HD)

    def go(ref, send, recv, device):
        remote(ref, ref, send, recv, device).start()

    first = pl.ds(0, FIRST)
    second = [pl.ds(FIRST + sum(GROUPS[:k]), GROUPS[k]) for k in range(len(GROUPS))]
    far_y = (4, 3, 5, 2, 6, 1, 7) if Y == 8 else tuple(range(1, Y))
    far_x = (2, 1, 3) if X == 4 else tuple(range(1, X))
    low, high = pl.ds(0, X // 2), pl.ds(X // 2, X // 2)

    def column(dy, some=slice(None)):
        return kv_buf.at[first, some, c, plus(y, dy, Y)]

    def line(k, dx):
        return kv_buf.at[second[k], plus(x, dx, X), c]

    def columns1(n):
        return kv_buf.at[first, :, 0, pl.ds(0, n)]

    def lines2(k, n):
        return kv_buf.at[second[k], pl.ds(0, n), 0]

    def share(ref, send, recv):
        if C > 1:
            go(ref, send, recv, sibling)

    def pushes2(k):
        return kv_buf.at[second[k], 0, 0, pl.ds(0, Y - 1)]

    def begin():
        for dx in far_x:
            go(kv_buf.at[first, x, c, y], x1_s, x1_r, x_at(dx))
        for k in range(len(GROUPS)):
            if k:
                wait(pushes2(k - 1), y2_s.at[k - 1])
            for dy in far_y:
                go(kv_buf.at[second[k], x, c, y], y2_s.at[k], y2_r.at[k], y_at(dy))

    def spread1():
        wait(kv_buf.at[first, pl.ds(0, X - 1), 0, 0], x1_r)
        for dy in (2, -2):
            go(column(0), y1_s.at[0], y1_r.at[0], y_at(dy))
        if not THROTTLE1:
            near1()
        share(column(0), c1_s, c1_r)

    def near1():
        if THROTTLE1:
            wait(columns1(2), y1_s.at[0])
        for dy in (1, -1):
            go(column(0), y1_s.at[1], y1_r.at[1], y_at(dy))

    def spread2(k):
        wait(pushes2(k), y2_r.at[k])
        for dx in far_x:
            go(line(k, 0), x2_s.at[k], x2_r.at[k, 1 if 2 * dx == X else 0], x_at(dx))
        share(line(k, 0), c2_s.at[k], c2_r.at[k])

    def forward1():
        wait(columns1(2), y1_r.at[0])
        for way, some in ((1, low), (-1, high)):
            go(column(-2 * way), y1_s.at[1], y1_r.at[2], y_at(way))
            go(column(-2 * way, some), y1_s.at[1], y1_r.at[3], y_at(2 * way))
        for dy in (2, -2):
            share(column(dy), c1_s, c1_r)
        wait(columns1(2), y1_r.at[1])
        for dy in (1, -1):
            share(column(dy), c1_s, c1_r)

    def finish1():
        wait(columns1(2), y1_r.at[2])
        for dy in (3, -3):
            share(column(dy), c1_s, c1_r)
        wait(columns1(1), y1_r.at[3])
        share(column(4), c1_s, c1_r)

    def finish2(k):
        near = [dx for dx in far_x if 2 * dx != X]
        if near:
            wait(lines2(k, len(near)), x2_r.at[k, 0])
        for dx in near:
            share(line(k, -dx), c2_s.at[k], c2_r.at[k])
        wait(lines2(k, 1), x2_r.at[k, 1])
        share(line(k, -X // 2), c2_s.at[k], c2_r.at[k])

    def complete():
        if C > 1:
            for k in range(len(GROUPS)):
                wait(lines2(k, X), c2_r.at[k])
            wait(columns1(Y), c1_r)

    scale = HD ** (-0.5)
    part = Z // 4
    keys_all = 2 * X * C * Y * 16

    def output(slot, j):
        dz = ORDER[slot]
        column = pl.ds(pl.multiple_of(j * HD, HD), HD)
        away = pl.ds(pl.multiple_of(z * cols + j * HD, HD), HD)
        src, dst = obuf.at[slot, :, column], o_hbm.at[:, away]
        if dz == 0:
            return pltpu.make_async_copy(src, dst, local_sem.at[3])
        return remote(src, dst, o_s, o_r, z_at(-dz))

    def attend(j, half):
        here = slice(half * part, (half + 1) * part)
        column = slice(j * HD, (j + 1) * HD)
        query = qbuf[here, :, column].reshape(part * tokens, HD)
        keys = [kv_buf[k * heads + j].reshape(keys_all // 2, HD) for k in (0, 1)]
        values = [kv_buf[k * heads + j].reshape(keys_all // 2, HD) for k in (2, 3)]
        values = [jnp.concatenate([v, jnp.ones_like(v)], axis=1) for v in values]
        across = (((1,), (1,)), ((), ()))
        peak, both = None, None
        for k in range(0, keys_all, CHUNK):
            part_of, at_row = divmod(k, keys_all // 2)
            rows = slice(at_row, at_row + CHUNK)
            scores = lax.dot_general(
                query, keys[part_of][rows], across, preferred_element_type=jnp.float32
            )
            new = jnp.max(scores, axis=1, keepdims=True)
            if k:
                new = jnp.maximum(peak, new)
            weights = jnp.exp((scores - new) * scale).astype(jnp.bfloat16)
            term = jnp.dot(weights, values[part_of][rows], preferred_element_type=jnp.float32)
            both = both * jnp.exp((peak - new) * scale) + term if k else term
            peak = new
        mixed = both[:, :HD] / both[:, HD:]
        power = jnp.mean(mixed * mixed, axis=1, keepdims=True)
        normed = (mixed * lax.rsqrt(power + EPS)).astype(jnp.bfloat16)
        obuf[here, :, column] = normed.reshape(part, tokens, HD)
        for slot in range(Z)[here]:
            output(slot, j).start()

    def queries_here():
        own_q.wait()
        wait(qbuf.at[pl.ds(0, Z - 1)], zq_r)

    steps = {
        "b": begin, "s": spread1, "t": spread2, "f": forward1, "e": finish1, "g": finish2, "n": near1,
        "c": complete,
    }
    for word in PLAN:
        if word != "n" or THROTTLE1:
            steps[word[0]](*(int(digit) for digit in word[1:]))
    queries_here()
    units = [(j, half) for j in range(heads) for half in range(4)]
    for j, half in units if HEADS_FIRST else sorted(units, key=lambda unit: unit[1]):
        attend(j, half)

    mine = obuf.at[SLOT[0]]
    wait(mine, local_sem.at[3])
    wait(obuf.at[pl.ds(0, Z - 1)], o_s)
    wait(obuf.at[pl.ds(0, Z - 1)], o_r)
    wait(send_kv.at[pl.ds(0, Z - 1)], zk_s)
    wait(qbuf.at[pl.ds(0, Z - 1)], zq_s)
    wait(kv_buf.at[first, pl.ds(0, X - 1), 0, 0], x1_s)
    if THROTTLE1:
        wait(columns1(5), y1_s.at[1])
    else:
        wait(columns1(2), y1_s.at[0])
        wait(columns1(5), y1_s.at[1])
    wait(pushes2(len(GROUPS) - 1), y2_s.at[len(GROUPS) - 1])
    for k in range(len(GROUPS)):
        wait(lines2(k, X - 1), x2_s.at[k])
        if C > 1:
            wait(lines2(k, X), c2_s.at[k])
    if C > 1:
        wait(columns1(Y), c1_s)


def shards(queries, keys, values):
    tokens, width = queries.shape
    cols = width // Z
    heads = cols // HD
    dma = pltpu.SemaphoreType.DMA
    bf16 = jnp.bfloat16
    return pl.pallas_call(
        kernel,
        out_shape=jax.ShapeDtypeStruct(queries.shape, bf16),
        in_specs=[pl.BlockSpec(memory_space=pltpu.HBM)] * 3,
        out_specs=pl.BlockSpec(memory_space=pl.ANY),
        scratch_shapes=[
            pltpu.VMEM((2 * tokens, width), bf16),
            pltpu.VMEM((Z, 32, HD), bf16),
            pltpu.VMEM((Z, 32, HD), bf16),
            pltpu.VMEM((4 * heads, X, C, Y, 16, HD), bf16),
            pltpu.VMEM((Z, tokens, cols), bf16),
            pltpu.VMEM((Z, tokens, cols), bf16),
        ]
        + [dma((4,))]
        + [dma] * 4
        + [dma((len(GROUPS),))] * 3
        + [dma((len(GROUPS), 2))]
        + [dma((len(GROUPS),))] * 2
        + [dma] * 2
        + [dma((2,)), dma((4,))]
        + [dma] * 4,
        compiler_params=pltpu.CompilerParams(
            collective_id=0, has_side_effects=True, vmem_limit_bytes=VMEM_BYTES
        ),
    )(queries, keys, values)


def solution(mesh):
    spec = P(("patch", "head"), None)
    return jax.shard_map(
        shards, mesh=mesh, in_specs=(spec, spec, spec), out_specs=spec, check_vma=False
    )
```
